32 devices in a mesh: row: 8 (over y, x, core), col: 4 (over z).
Axes of the slice: x: 2, y: 2, z: 4, core: 2. Of those that a mesh axis runs over, the one named last changes fastest.
Arguments:
- p_cov: float32 [8192, 8192], P('row', 'col'), as said below
- a_blocks: float32 [64, 16, 128, 128], P('row'), may hold values from -0.15625 to 0.15625
- pattern: int32 [64, 16], P('row'), may hold values from -1 to 63, as said below
- q_diag: float32 [8192], P('row'), may hold values from 0.2 to 2
Outputs:
- p_next: float32 [8192, 8192], P('row', 'col')
The draws below stay inside these ranges and needn't reach their ends.
Inputs may be any that keep to these rules, and one draw needn't show every extreme that they name: p_cov is exactly symmetric. `pattern`: in each row i the entries that are not -1 are distinct, lie within 8 of i, include i itself and fill the leading slots; some row uses all 16 slots.
All inputs are finite; a program needn't handle non-finite values.
Results may differ from the reference program's by a relative error of at most 0.0003.
Values sent between devices are 32-bit elements; how exact they have to be, the bound alone decides.
No kernel may reach another device: no remote copies, remote signals or barrier semaphores. Data moves between devices by JAX's collectives and lax.ppermute only.
A program may use at most 192 MiB of HBM per device.

```python
import math
import jax
import jax.numpy as jnp
from jax import lax

NB = 64
BS = 128
KMAX = 16
REACH = 8
N = 8192


def draw_p_cov(key, part):
    order = NB * BS
    key_normal = jax.random.fold_in(jax.random.fold_in(key, 7), 0)
    raw = jax.random.normal(key_normal, (order, order), jnp.float32)
    symmetric = 0.5 * (raw + raw.T)
    return symmetric + 2.0 * jnp.eye(order, dtype=jnp.float32)


def draw_pattern(key, part):
    key_score, key_count, key_full = jax.random.split(jax.random.fold_in(key, 11), 3)
    width = 2 * REACH + 1
    row_ids = jnp.arange(NB, dtype=jnp.int32)[:, None]
    offsets = jnp.arange(width, dtype=jnp.int32)[None, :] - REACH
    candidate = row_ids + offsets
    valid = (candidate >= 0) & (candidate < NB)
    scores = jax.random.randint(key_score, (NB, width), 0, 1 << 20) * 64 + jnp.arange(width, dtype=jnp.int32)[None, :]
    scores = jnp.where(offsets == 0, -1, scores)
    scores = jnp.where(valid, scores, 1 << 29)
    unused, order_idx = jax.lax.top_k(-scores, KMAX)
    counts = jax.random.randint(key_count, (NB,), KMAX // 2, KMAX + 1)
    full_row = jax.random.randint(key_full, (), REACH, NB - REACH)
    counts = jnp.where(jnp.arange(NB, dtype=jnp.int32) == full_row, KMAX, counts)
    chosen_off = jnp.take(offsets[0], order_idx)
    chosen = row_ids + chosen_off
    chosen_ok = jnp.take_along_axis(valid, order_idx, axis=1)
    slot_ids = jnp.arange(KMAX, dtype=jnp.int32)[None, :]
    keep = (slot_ids < counts[:, None]) & chosen_ok
    return jnp.where(keep, chosen, -1).astype(jnp.int32)


def block_levels(stream_key, extent, cuts, low, high):
    factor_of, own = 1.0, jax.random.fold_in(stream_key, 6)
    for position, parts in cuts:
        steps = jnp.exp(jax.random.uniform(jax.random.fold_in(own, position), (parts,), jnp.float32, low / len(cuts), high / len(cuts)))
        factor_of = factor_of * jnp.repeat(steps, extent[position] // parts).reshape([-1 if axis == position else 1 for axis in range(len(extent))])
    return factor_of


def centred(own_key, extent, scale, reach, pieces=(), held_as=jnp.bfloat16):
    entries = scale * jax.random.normal(own_key, extent, jnp.float32)
    if pieces:
        entries = entries * block_levels(own_key, extent, pieces, -0.22, 0.18)
    return jnp.clip(entries, -reach, reach).astype(held_as)


def setup_inputs(seed: int = 0) -> dict:
    key_list = jax.random.split(jax.random.key(seed), 5)
    return {
        "p_cov": draw_p_cov(jax.random.fold_in(key_list[4], 71), 0),
        "a_blocks": centred(key_list[1], (NB, KMAX, BS, BS), (BS * 12) ** -0.5, 0.15625, ((0, 8),), jnp.float32),
        "pattern": draw_pattern(jax.random.fold_in(key_list[4], 71), 0),
        "q_diag": jnp.clip(jnp.exp(math.log(2.0) - 2.3025851 * jax.random.uniform(key_list[3], (N,), jnp.float32) ** block_levels(key_list[3], (N,), ((0, 8),), -0.2, 0.2)), 0.2, 2.0),
    }


time_step = 0.25


def apply_jacobian(p_full, a_blocks, pattern):
    stacked = p_full.reshape(NB, BS, NB * BS)

    def one_row(index):
        slots = pattern[index]
        safe = jnp.clip(slots, 0, NB - 1).astype(jnp.int32)
        picked = stacked[safe]
        weights = a_blocks[index] * (slots >= 0).astype(a_blocks.dtype)[:, None, None]
        return jnp.einsum("sxy,syn->xn", weights, picked, precision=lax.Precision.HIGHEST)

    return lax.map(one_row, jnp.arange(NB, dtype=jnp.int32)).reshape(NB * BS, NB * BS)


def reference(p_cov, a_blocks, pattern, q_diag):
    noise = jnp.diag(q_diag)

    def tendency(p_full):
        product = apply_jacobian(p_full, a_blocks, pattern)
        return product + product.T + noise

    k_first = tendency(p_cov)
    p_mid = p_cov + time_step * k_first
    k_second = tendency(p_mid)
    return p_cov + (0.5 * time_step) * (k_first + k_second)
```

```python
import functools

import jax
import jax.numpy as jnp
from jax import lax
from jax.experimental import pallas as pl
from jax.experimental.pallas import tpu as pltpu
from jax.sharding import PartitionSpec as P

BS = 128
REACH = 8
HALO = REACH * BS
TILE = 2 * BS
WIDE = TILE + 2 * HALO
CHUNKS = 2

time_step = 0.25

VMEM_BYTES = 56 * 1024 * 1024


def shifted(array, axis, by):
    peers = lax.axis_size(axis)
    pairs = [(i, i + by) for i in range(peers) if 0 <= i + by < peers]
    return lax.ppermute(array, axis, pairs)


def broadcast(value, axis, source):
    kept = jnp.where(lax.axis_index(axis) == source, value, 0).astype(value.dtype)
    return lax.psum(kept, axis)


def with_halo(block, sides, width):
    for axis, dim in sides:
        count = lax.axis_size(axis)
        forward = [(i, i + 1) for i in range(count - 1)]
        backward = [(target, source) for source, target in forward]
        low = lax.ppermute(
            lax.slice_in_dim(block, block.shape[dim] - width, None, axis=dim), axis, forward
        )
        high = lax.ppermute(lax.slice_in_dim(block, 0, width, axis=dim), axis, backward)
        block = jnp.concatenate([low, block, high], axis=dim)
    return block


def band_matrix(blocks, slots, first_block, extent):
    picks = jnp.arange(extent, dtype=jnp.int32)[None, None, :]
    onehot = ((slots - first_block)[:, :, None] == picks).astype(jnp.float32)
    banded = jnp.einsum("bse,bsxy->bxey", onehot, blocks, precision=lax.Precision.HIGHEST)
    return banded.reshape(blocks.shape[0] * BS, extent * BS)


def general_body(p_cov, a_blocks, pattern, q_diag):
    rows_dev, cols_dev = p_cov.shape
    row_count = lax.axis_size("row")
    col_count = lax.axis_size("col")
    row_idx = lax.axis_index("row")
    col_idx = lax.axis_index("col")
    row_blocks = rows_dev // BS
    span_devs = REACH * BS // rows_dev
    group_rows = row_count // col_count
    global_rows = row_idx * rows_dev + jnp.arange(rows_dev, dtype=jnp.int32)[:, None]
    global_cols = col_idx * cols_dev + jnp.arange(cols_dev, dtype=jnp.int32)[None, :]
    noise_term = jnp.where(global_rows == global_cols, q_diag[:, None], 0.0)
    row_band = band_matrix(
        a_blocks,
        pattern,
        row_idx * row_blocks - span_devs * row_blocks,
        (2 * span_devs + 1) * row_blocks,
    )

    def forward(p_local):
        pieces = []
        for offset in range(-span_devs, span_devs + 1):
            if offset == 0:
                pieces.append(p_local)
            else:
                pieces.append(shifted(p_local, "row", -offset))
        extended = jnp.concatenate(pieces, axis=0)
        return jnp.dot(
            row_band, extended, precision=lax.Precision.HIGHEST, preferred_element_type=jnp.float32
        )

    fetched_blocks = []
    fetched_slots = []
    for member in range(group_rows):
        got_blocks, got_slots = (
            broadcast(a_blocks, "row", col_idx * group_rows + member),
            broadcast(pattern.astype(jnp.float32), "row", col_idx * group_rows + member),
        )
        fetched_blocks.append(got_blocks)
        fetched_slots.append(got_slots)
    col_blocks = jnp.concatenate(fetched_blocks, axis=0)
    col_slots = jnp.concatenate(fetched_slots, axis=0).astype(jnp.int32)
    col_band = band_matrix(
        col_blocks, col_slots, col_idx * (cols_dev // BS) - REACH, cols_dev // BS + 2 * REACH
    )

    def tendency(p_local):
        product = forward(p_local)
        widened = with_halo(p_local, (("col", 1),), REACH * BS)
        other = lax.dot_general(
            widened,
            col_band,
            (((1,), (1,)), ((), ())),
            precision=lax.Precision.HIGHEST,
            preferred_element_type=jnp.float32,
        )
        return product + other + noise_term

    k_first = tendency(p_cov)
    p_mid = p_cov + time_step * k_first
    k_second = tendency(p_mid)
    return p_cov + 0.5 * time_step * (k_first + k_second)


def split(values):
    high = values.astype(jnp.bfloat16)
    return high, (values - high.astype(jnp.float32)).astype(jnp.bfloat16)


def product(left_high, left_low, right_high, right_low):
    dot = functools.partial(jnp.dot, preferred_element_type=jnp.float32)
    return dot(left_high, right_high) + (dot(left_high, right_low) + dot(left_low, right_high))


def params():
    return pltpu.CompilerParams(vmem_limit_bytes=VMEM_BYTES)


def cost(flops, bytes_accessed):
    return pl.CostEstimate(flops=flops // 64, bytes_accessed=bytes_accessed // 64, transcendentals=0)


def pick_kernel(role, *refs):
    *sources, out = refs
    for index, source in enumerate(sources):

        @pl.when(role[0] == index)
        def _(source=source):
            out[...] = source[...]


def pick(role, *sources):
    shape = sources[0].shape
    block = (1, shape[1] // 2, *shape[2:])

    def spec(index):
        def place(i, role):
            here = jnp.where(role[0] == index, i, 0)
            return (here // 2, lax.rem(here, 2), 0, 0)

        return pl.BlockSpec(block, place)

    return pl.pallas_call(
        pick_kernel,
        grid_spec=pltpu.PrefetchScalarGridSpec(
            num_scalar_prefetch=1,
            grid=(2 * shape[0],),
            in_specs=[spec(index) for index in range(len(sources))],
            out_specs=pl.BlockSpec(block, lambda i, role: (i // 2, lax.rem(i, 2), 0, 0)),
        ),
        out_shape=jax.ShapeDtypeStruct(shape, sources[0].dtype),
        compiler_params=params(),
        cost_estimate=cost(0, sources[0].size * 8),
    )(role, *sources)


def row_band_kernel(slots, place, blocks, near_high, near_low, far_high, far_low):
    pair = pl.program_id(0)
    for ref in (near_high, near_low, far_high, far_low):
        ref[...] = jnp.zeros_like(ref)
    blocks_dev = HALO // BS
    for half in range(TILE // BS):
        rows = pl.ds(half * BS, BS)
        for slot in range(blocks.shape[1]):
            column = slots[pair * 2 + half, slot]
            at = column - place[0]
            far_at = jnp.where(place[1] == 0, at + blocks_dev, at - blocks_dev)
            is_far = (far_at >= 0) & (far_at < blocks_dev)

            @pl.when((column >= 0) & is_far)
            def _(half=half, slot=slot, far_at=far_at, rows=rows):
                lanes = pl.ds(pl.multiple_of(far_at * BS, BS), BS)
                far_high[0, rows, lanes], far_low[0, rows, lanes] = split(blocks[half, slot])

            @pl.when((column >= 0) & jnp.logical_not(is_far))
            def _(half=half, slot=slot, at=at, rows=rows):
                lanes = pl.ds(pl.multiple_of((at + place[1] * blocks_dev) * BS, BS), BS)
                near_high[0, rows, lanes], near_low[0, rows, lanes] = split(blocks[half, slot])


def row_bands(a_blocks, pattern, place):
    count, slots = pattern.shape
    tiles = count * BS // TILE
    outs = [jax.ShapeDtypeStruct((tiles, TILE, width), jnp.bfloat16) for width in (2 * HALO, HALO)]
    specs = [pl.BlockSpec((1, TILE, width), lambda i, *_: (i, 0, 0)) for width in (2 * HALO, HALO)]
    got = pl.pallas_call(
        row_band_kernel,
        grid_spec=pltpu.PrefetchScalarGridSpec(
            num_scalar_prefetch=2,
            grid=(tiles,),
            in_specs=[pl.BlockSpec((2, slots, BS, BS), lambda i, *_: (i, 0, 0, 0))],
            out_specs=[specs[0], specs[0], specs[1], specs[1]],
        ),
        out_shape=[outs[0], outs[0], outs[1], outs[1]],
        compiler_params=params(),
        cost_estimate=cost(0, a_blocks.size * 4 + tiles * TILE * 3 * HALO * 4),
    )(pattern, place, a_blocks)
    return got[:2], got[2:]


def col_band_kernel(slots, base, core, mine, other, *refs, per_core):
    high, low = refs[-2:]
    step = pl.program_id(0)
    half_rows = slots.shape[0] // 2
    owner = step // per_core
    pair = lax.rem(step, per_core)
    high[...] = jnp.zeros_like(high)
    low[...] = jnp.zeros_like(low)
    for mine_here, blocks in ((True, mine), (False, other)):

        @pl.when((core[0] == owner) == mine_here)
        def _(blocks=blocks):
            for half in range(TILE // BS):
                rows = pl.ds(half * BS, BS)
                for slot in range(blocks.shape[1]):
                    column = slots[owner * half_rows + pair * 2 + half, slot]

                    @pl.when(column >= 0)
                    def _(rows=rows, half=half, slot=slot, column=column):
                        place = column - base[owner] - 2 * pair + REACH
                        lanes = pl.ds(pl.multiple_of(place * BS, BS), BS)
                        high[0, rows, lanes], low[0, rows, lanes] = split(blocks[half, slot])


def col_bands(mine, other, slots, base, core, chunk, into):
    count, width = slots.shape
    per_core = count * BS // TILE // 2
    tiles = 2 * per_core * CHUNKS
    out = jax.ShapeDtypeStruct((tiles, TILE, WIDE), jnp.bfloat16)

    def tile(i, *_):
        return (i // per_core * (tiles // 2) + chunk * per_core + lax.rem(i, per_core), 0, 0)

    blocks = pl.BlockSpec((2, width, BS, BS), lambda i, *_: (lax.rem(i, per_core), 0, 0, 0))
    spec = pl.BlockSpec((1, TILE, WIDE), tile)
    return pl.pallas_call(
        functools.partial(col_band_kernel, per_core=per_core),
        grid_spec=pltpu.PrefetchScalarGridSpec(
            num_scalar_prefetch=3,
            grid=(2 * per_core,),
            in_specs=[blocks, blocks] + [pl.BlockSpec(memory_space=pl.ANY)] * len(into),
            out_specs=[spec, spec],
        ),
        out_shape=[out, out],
        input_output_aliases={5: 0, 6: 1} if into else {},
        compiler_params=params(),
        cost_estimate=cost(0, mine.size * 16 + tiles * TILE * WIDE * 4),
    )(slots, base, core, mine, other, *into)


def resident(array):
    return pl.BlockSpec(array.shape, lambda *_: (0,) * array.ndim, pipeline_mode=pl.Buffered(1))


def near_kernel(core, band_high, band_low, own, sibling, *refs, scale):
    *bases, out, ext_high, ext_low = refs
    rows = own.shape[0]
    part = rows // max(len(bases), 1)

    def place(own_at, sibling_at):
        for at, ref in ((own_at, own), (sibling_at, sibling)):
            ext_high[pl.ds(at, rows), :], ext_low[pl.ds(at, rows), :] = split(ref[...])

    def multiply(tile, reach):
        got = product(
            band_high[tile, :, reach],
            band_low[tile, :, reach],
            ext_high[reach, :],
            ext_low[reach, :],
        )
        got = scale * got
        at = tile * TILE
        if bases:
            got += bases[at // part][pl.ds(at % part, TILE), :]
        out[pl.ds(at, TILE), :] = got

    @pl.when(core[0] == 0)
    def _():
        place(0, rows)
        for tile in range(rows // TILE):
            multiply(tile, slice(0, HALO + (tile + 1) * TILE))

    @pl.when(core[0] == 1)
    def _():
        place(rows, 0)
        for tile in range(rows // TILE):
            multiply(tile, slice(tile * TILE, HALO + rows))


def near(core, bands, own, sibling, scale, bases=(), place=0, lanes=512):
    rows, cols = own.shape
    start = place // lanes
    spec = pl.BlockSpec((rows, lanes), lambda i, *_: (0, i))
    base = pl.BlockSpec((rows // max(len(bases), 1), lanes), lambda i, *_: (0, i + start))
    return pl.pallas_call(
        functools.partial(near_kernel, scale=scale),
        grid_spec=pltpu.PrefetchScalarGridSpec(
            num_scalar_prefetch=1,
            grid=(cols // lanes,),
            in_specs=[resident(bands[0]), resident(bands[1]), spec, spec] + [base] * len(bases),
            out_specs=spec,
            scratch_shapes=[pltpu.VMEM((2 * rows, lanes), jnp.bfloat16)] * 2,
        ),
        out_shape=jax.ShapeDtypeStruct((rows, cols), jnp.float32),
        compiler_params=params(),
        cost_estimate=cost(6 * rows * cols * 1664, 3 * rows * cols * 4),
    )(core, *bands, own, sibling, *bases)


def diagonal(noise, shape, row_at, col_at):
    row = lax.broadcasted_iota(jnp.int32, shape, 0) + row_at
    col = lax.broadcasted_iota(jnp.int32, shape, 1) + col_at
    return jnp.where(row == col, noise, 0.0)


def far_kernel(where, band_high, band_low, far, relayed, noise, *refs, scale, add_noise):
    *bases, out, far_high, far_low = refs
    rows, lanes = far.shape
    part = rows // len(bases)

    @pl.when(where[2] == 0)
    def _():
        far_high[...], far_low[...] = split(far[...])

    @pl.when(where[2] == 1)
    def _():
        far_high[...], far_low[...] = split(relayed[...])

    def multiply(tile, reach):
        got = product(
            band_high[tile, :, reach],
            band_low[tile, :, reach],
            far_high[reach, :],
            far_low[reach, :],
        )
        at = tile * TILE
        base = bases[at // part][pl.ds(at % part, TILE), :]
        out[pl.ds(at, TILE), :] = base + scale * got

    @pl.when(where[0] == 0)
    def _():
        for tile in range(rows // TILE):
            multiply(tile, slice(tile * TILE, rows))

    @pl.when(where[0] == 1)
    def _():
        for tile in range(rows // TILE):
            multiply(tile, slice(0, (tile + 1) * TILE))

    if add_noise:
        shift = where[1] + pl.program_id(0) * lanes

        @pl.when((shift < rows) & (shift + lanes > 0))
        def _():
            for tile in range(rows // TILE):
                span = pl.ds(tile * TILE, TILE)
                out[span, :] += time_step * diagonal(noise[span, :], (TILE, lanes), tile * TILE, shift)


def far_part(where, bands, far, noise, bases, place, scale, add_noise, in_place=False, lanes=256):
    straight, relayed = far
    rows, cols = straight.shape
    start = place // lanes
    base = pl.BlockSpec((rows // len(bases), lanes), lambda i, *_: (0, i + start))
    out = base if in_place else pl.BlockSpec((rows, lanes), lambda i, *_: (0, i))

    def source(relay):
        return pl.BlockSpec((rows, lanes), lambda i, where: (0, jnp.where(where[2] == relay, i, 0)))

    return pl.pallas_call(
        functools.partial(far_kernel, scale=scale, add_noise=add_noise),
        grid_spec=pltpu.PrefetchScalarGridSpec(
            num_scalar_prefetch=1,
            grid=(cols // lanes,),
            in_specs=[resident(bands[0]), resident(bands[1]), source(0), source(1), resident(noise)]
            + [base] * len(bases),
            out_specs=out,
            scratch_shapes=[pltpu.VMEM((rows, lanes), jnp.bfloat16)] * 2,
        ),
        out_shape=jax.ShapeDtypeStruct(bases[0].shape if in_place else (rows, cols), jnp.float32),
        input_output_aliases={6: 0} if in_place else {},
        compiler_params=params(),
        cost_estimate=cost(6 * rows * cols * 640, 3 * rows * cols * 4),
    )(where, *bands, straight, relayed, noise, *bases)


def right_product(bands, pieces, ext_high, ext_low):
    step = pl.program_id(0)

    @pl.when(step == 0)
    def _():
        at = 0
        for piece in pieces:
            span = pl.ds(at, piece.shape[1])
            ext_high[:, span], ext_low[:, span] = split(piece[...])
            at += piece.shape[1]

    dot = functools.partial(
        lax.dot_general,
        dimension_numbers=(((1,), (1,)), ((), ())),
        preferred_element_type=jnp.float32,
    )
    reach = pl.ds(pl.multiple_of(step * TILE, TILE), WIDE)
    high, low = ext_high[:, reach], ext_low[:, reach]
    band_high, band_low = bands
    return dot(high, band_high) + (dot(high, band_low) + dot(low, band_high))


def right_first_kernel(where, *refs, half_cols):
    high, low, low_side, own, high_side, p_tile, m_low, m_high, e_low, e_high, noise = refs[:11]
    w_low, w_high, base, ext_high, ext_low = refs[11:]
    step = pl.program_id(0)
    rows, lanes = p_tile.shape
    v = time_step * right_product((high[0], low[0]), (low_side, own, high_side), ext_high, ext_low)
    shift = where[1] + step * lanes
    for here, m_tile, extra, w in ((0, m_low, e_low, w_low), (1, m_high, e_high, w_high)):

        @pl.when(step // half_cols == here)
        def _(m_tile=m_tile, extra=extra, w=w):
            base[...] = (p_tile[...] + extra[...]) + (m_tile[...] + v)
            w[...] = m_tile[...] + 0.5 * v

            @pl.when((shift < rows) & (shift + lanes > 0))
            def _():
                w[...] -= (0.5 * time_step) * diagonal(noise[...], (rows, lanes), 0, shift)


def right_specs(rows, part, half_cols):
    def whole(width):
        return pl.BlockSpec((rows, width), lambda i, *_: (part, 0), pipeline_mode=pl.Buffered(1))

    full = pl.BlockSpec((rows, TILE), lambda i, *_: (part, i))
    first = pl.BlockSpec((rows, TILE), lambda i, *_: (part, jnp.minimum(i, half_cols - 1)))
    second = pl.BlockSpec((rows, TILE), lambda i, *_: (part, jnp.maximum(i - half_cols, 0)))
    return whole, full, first, second


BAND = pl.BlockSpec((1, TILE, WIDE), lambda i, *_: (i, 0, 0))


def right_first(where, bands, p, sides, m, extra, noise, part, parts):
    rows, cols = p.shape
    rows //= parts
    half_cols = cols // TILE // 2
    whole, full, first, second = right_specs(rows, part, half_cols)
    _, out_full, out_first, out_second = right_specs(rows, 0, half_cols)
    half = jax.ShapeDtypeStruct((rows, cols // 2), jnp.float32)
    return pl.pallas_call(
        functools.partial(right_first_kernel, half_cols=half_cols),
        grid_spec=pltpu.PrefetchScalarGridSpec(
            num_scalar_prefetch=1,
            grid=(cols // TILE,),
            in_specs=[BAND, BAND, whole(HALO), whole(cols), whole(HALO), full]
            + [first, second, first, second, whole(1)],
            out_specs=[out_first, out_second, out_full],
            scratch_shapes=[pltpu.VMEM((rows, cols + 2 * HALO), jnp.bfloat16)] * 2,
        ),
        out_shape=[half, half, jax.ShapeDtypeStruct((rows, cols), jnp.float32)],
        compiler_params=params(),
        cost_estimate=cost(6 * rows * cols * WIDE, 5 * rows * cols * 4),
    )(where, *bands, sides[0], p, sides[1], p, *m, *extra, noise)


def right_last_kernel(high, low, low_side, w_low, w_high, high_side, g_low, g_high, *refs, half_cols):
    out, ext_high, ext_low = refs[-3:]
    pieces = (low_side, w_low, w_high, high_side)
    got = time_step * right_product((high[0], low[0]), pieces, ext_high, ext_low)
    for here, g in ((0, g_low), (1, g_high)):

        @pl.when(pl.program_id(0) // half_cols == here)
        def _(g=g):
            out[...] = g[...] + got


def right_last(bands, w, sides, g, base, into, part, parts):
    rows, half = w[0].shape
    half_cols = half // TILE
    whole, _, _, _ = right_specs(rows, 0, half_cols)
    _, full, first, _ = right_specs(rows, part, half_cols)
    second = pl.BlockSpec((rows, TILE), lambda i: (0, jnp.maximum(i, half_cols)))
    prior = [] if into is None else [into]
    return pl.pallas_call(
        functools.partial(right_last_kernel, half_cols=half_cols),
        grid=(2 * half_cols,),
        in_specs=[BAND, BAND, whole(HALO), whole(half), whole(half), whole(HALO), first, second]
        + [pl.BlockSpec(memory_space=pl.ANY)] * len(prior),
        out_specs=full,
        scratch_shapes=[pltpu.VMEM((rows, 2 * (half + HALO)), jnp.bfloat16)] * 2,
        out_shape=jax.ShapeDtypeStruct((rows * parts, 2 * half), jnp.float32),
        input_output_aliases={8: 0} if prior else {},
        compiler_params=params(),
        cost_estimate=cost(6 * rows * 2 * half * WIDE, 5 * rows * 2 * half * 4),
    )(*bands, sides[0], *w, sides[1], g, base, *prior)


def permute(array, moves):
    return lax.ppermute(array, "row", moves)


def permute_by_column(array, moves):
    cols = lax.axis_size("col")
    pairs = [
        (source * cols + col, target * cols + col)
        for col in range(cols)
        for source, target in moves(col)
    ]
    return lax.ppermute(array, ("row", "col"), pairs)


def dev(chip, core):
    return 2 * chip + core


def after(value, *others):
    return lax.optimization_barrier((value, *others))[0]


def off_chip_rows(x):
    count = lax.axis_size("row")
    moves = []
    for low in range(1, count - 1, 2):
        moves += [(low, low + 1), (low + 1, low)]
    straight = [pair for pair in moves if set(pair) != {dev(1, 1), dev(2, 0)}]
    first = permute(x[0], moves)
    hop = permute(x[1], [(dev(1, 1), dev(3, 1)), (dev(2, 0), dev(0, 0))])
    second = permute(x[1], straight)
    landed = permute(hop, [(dev(3, 1), dev(2, 0)), (dev(0, 0), dev(1, 1))])
    return (first, first), (second, landed)


def sides(low_half, high_half):
    cols = lax.axis_size("col")
    low_side = lax.ppermute(high_half, "col", [(i, i + 1) for i in range(cols - 1)])
    high_side = lax.ppermute(low_half, "col", [(i + 1, i) for i in range(cols - 1)])
    return low_side, high_side


def halves(x):
    middle = x.shape[1] // 2
    return lax.slice_in_dim(x, 0, middle, axis=1), lax.slice_in_dim(x, middle, None, axis=1)


def paired_body(p_cov, a_blocks, pattern, q_diag):
    rows_dev, cols_dev = p_cov.shape
    row = lax.axis_index("row")
    col = lax.axis_index("col")
    chip = row // 2
    at_core = lax.rem(row, 2)
    core = jnp.full((1,), at_core, jnp.int32)
    relayed = ((row == dev(1, 1)) | (row == dev(2, 0))).astype(jnp.int32)
    offset = col * cols_dev - row * rows_dev
    where = [
        jnp.stack([at_core, offset + half * HALO, relayed * half]).astype(jnp.int32)
        for half in (0, 1)
    ]
    count = lax.axis_size("row")
    swap = [(i, i ^ 1) for i in range(count)]
    noise = q_diag.reshape(rows_dev, 1)
    col_count = cols_dev // BS

    all_slots = lax.all_gather(pattern, "row", axis=0, tiled=True)
    place = jnp.stack([row * (rows_dev // BS), at_core]).astype(jnp.int32)
    near_bands, far_bands = row_bands(a_blocks, pattern, place)

    p_sent = after(p_cov, all_slots)
    sibling = permute(p_sent, swap)
    p = halves(p_sent)
    p_far = off_chip_rows(p)
    p_sides = sides(*p)
    m_near = near(core, near_bands, p_cov, sibling, time_step)

    def far_of_p(h, far):
        return far_part(where[h], far_bands, far, noise, [m_near], h * HALO, time_step, True)

    away = chip ^ col
    by_core = jnp.array([[0, 1, 2, 3], [0, 4, 1, 3]], jnp.int32)
    role = by_core[at_core, away].reshape(1)
    size = a_blocks.shape[0] // CHUNKS
    owns = [lax.slice_in_dim(a_blocks, k * size, (k + 1) * size, axis=0) for k in range(CHUNKS)]
    owns = [after(own, all_slots) for own in owns]
    ones = [
        permute_by_column(own, lambda c: [(dev(c, 0), dev(c ^ 1, 0)), (dev(c, 1), dev(c ^ 2, 1))])
        for own in owns
    ]
    twos = [permute_by_column(own, lambda c: [(dev(c, 0), dev(c ^ 2, 0))]) for own in owns]
    ones = [after(ones[0], sibling), after(ones[1], m_near)]
    seconds = [
        permute_by_column(
            one, lambda c: [(dev(c ^ 1, 0), dev(c ^ 3, 0)), (dev(c ^ 2, 1), dev(c ^ 3, 1))]
        )
        for one in ones
    ]
    thirds = [
        permute_by_column(second, lambda c: [(dev(c ^ 3, 1), dev(c ^ 1, 1))])
        for second in (after(seconds[0], m_near), seconds[1])
    ]
    p_far = [
        [after(part, *held) for part in parts]
        for parts, held in zip(p_far, (seconds[:1], (thirds[0], *twos, *p_sides)))
    ]
    m = [far_of_p(h, p_far[h]) for h in (0, 1)]
    m_sibling = [permute(part, swap) for part in m]
    m_far = off_chip_rows(m)
    half_step = 0.5 * time_step
    m_twice = [near(core, near_bands, m[h], m_sibling[h], half_step) for h in (0, 1)]

    (m_first, _), (m_second, m_landed) = m_far
    forced_mine = ((m[0],), (m[1],))
    mines, others = [], []
    for chunk in range(CHUNKS):
        own = after(owns[chunk], *forced_mine[chunk])
        mines.append(pick(role, own, ones[chunk], twos[chunk], seconds[chunk], thirds[chunk]))
        others.append(permute(mines[chunk], swap))
    bands = ()
    for chunk in range(CHUNKS):
        first_rows = [col * col_count + half * (col_count // 2) + chunk * size for half in (0, 1)]
        slots = jnp.concatenate(
            [lax.dynamic_slice_in_dim(all_slots, row_at, size, axis=0) for row_at in first_rows], axis=0
        )
        base = jnp.stack(first_rows).astype(jnp.int32)
        bands = col_bands(mines[chunk], others[chunk], slots, base, core, chunk, bands)

    parts = 2
    got = []
    for part in range(parts):
        shift = where[0] - jnp.array([0, part * (rows_dev // parts), 0], jnp.int32)
        noise_then = after(noise, m_first) if part else noise
        got.append(right_first(shift, bands, p_cov, p_sides, m, m_twice, noise_then, part, parts))
    w_sides = [sides(w_low, w_high) for w_low, w_high, _ in got]
    w_sides[0] = [after(side, m_landed) for side in w_sides[0]]
    bases = [base for _, _, base in got]
    g = far_part(where[0], far_bands, m_far[0], noise, bases, 0, half_step, False)
    out = None
    for part in range(parts):
        out = right_last(bands, got[part][:2], w_sides[part], g, bases[part], out, part, parts)
    return far_part(where[1], far_bands, m_far[1], noise, [out], HALO, half_step, False, True)


def solution(mesh):
    def body(p_cov, a_blocks, pattern, q_diag):
        rows_dev, cols_dev = p_cov.shape
        rows, cols = lax.axis_size("row"), lax.axis_size("col")
        paired = rows == 8 and cols == 4 and rows_dev == HALO and cols_dev == 2 * HALO
        return (paired_body if paired else general_body)(p_cov, a_blocks, pattern, q_diag)

    return jax.shard_map(
        body,
        mesh=mesh,
        in_specs=(P("row", "col"), P("row", None, None, None), P("row", None), P("row")),
        out_specs=P("row", "col"),
        check_vma=False,
    )
```

```python
import functools

import jax
import jax.numpy as jnp
from jax import lax
from jax.experimental import pallas as pl
from jax.experimental.pallas import tpu as pltpu
from jax.sharding import PartitionSpec as P

BS = 128
REACH = 8
HALO = REACH * BS
TILE = 2 * BS
WIDE = TILE + 2 * HALO
CHUNKS = 2

time_step = 0.25

VMEM_BYTES = 56 * 1024 * 1024


def shifted(array, axis, by):
    peers = lax.axis_size(axis)
    pairs = [(i, i + by) for i in range(peers) if 0 <= i + by < peers]
    return lax.ppermute(array, axis, pairs)


def broadcast(value, axis, source):
    kept = jnp.where(lax.axis_index(axis) == source, value, 0).astype(value.dtype)
    return lax.psum(kept, axis)


def with_halo(block, sides, width):
    for axis, dim in sides:
        count = lax.axis_size(axis)
        forward = [(i, i + 1) for i in range(count - 1)]
        backward = [(target, source) for source, target in forward]
        low = lax.ppermute(
            lax.slice_in_dim(block, block.shape[dim] - width, None, axis=dim), axis, forward
        )
        high = lax.ppermute(lax.slice_in_dim(block, 0, width, axis=dim), axis, backward)
        block = jnp.concatenate([low, block, high], axis=dim)
    return block


def band_matrix(blocks, slots, first_block, extent):
    picks = jnp.arange(extent, dtype=jnp.int32)[None, None, :]
    onehot = ((slots - first_block)[:, :, None] == picks).astype(jnp.float32)
    banded = jnp.einsum("bse,bsxy->bxey", onehot, blocks, precision=lax.Precision.HIGHEST)
    return banded.reshape(blocks.shape[0] * BS, extent * BS)


def general_body(p_cov, a_blocks, pattern, q_diag):
    rows_dev, cols_dev = p_cov.shape
    row_count = lax.axis_size("row")
    col_count = lax.axis_size("col")
    row_idx = lax.axis_index("row")
    col_idx = lax.axis_index("col")
    row_blocks = rows_dev // BS
    span_devs = REACH * BS // rows_dev
    group_rows = row_count // col_count
    global_rows = row_idx * rows_dev + jnp.arange(rows_dev, dtype=jnp.int32)[:, None]
    global_cols = col_idx * cols_dev + jnp.arange(cols_dev, dtype=jnp.int32)[None, :]
    noise_term = jnp.where(global_rows == global_cols, q_diag[:, None], 0.0)
    row_band = band_matrix(
        a_blocks,
        pattern,
        row_idx * row_blocks - span_devs * row_blocks,
        (2 * span_devs + 1) * row_blocks,
    )

    def forward(p_local):
        pieces = []
        for offset in range(-span_devs, span_devs + 1):
            if offset == 0:
                pieces.append(p_local)
            else:
                pieces.append(shifted(p_local, "row", -offset))
        extended = jnp.concatenate(pieces, axis=0)
        return jnp.dot(
            row_band, extended, precision=lax.Precision.HIGHEST, preferred_element_type=jnp.float32
        )

    fetched_blocks = []
    fetched_slots = []
    for member in range(group_rows):
        got_blocks, got_slots = (
            broadcast(a_blocks, "row", col_idx * group_rows + member),
            broadcast(pattern.astype(jnp.float32), "row", col_idx * group_rows + member),
        )
        fetched_blocks.append(got_blocks)
        fetched_slots.append(got_slots)
    col_blocks = jnp.concatenate(fetched_blocks, axis=0)
    col_slots = jnp.concatenate(fetched_slots, axis=0).astype(jnp.int32)
    col_band = band_matrix(
        col_blocks, col_slots, col_idx * (cols_dev // BS) - REACH, cols_dev // BS + 2 * REACH
    )

    def tendency(p_local):
        product = forward(p_local)
        widened = with_halo(p_local, (("col", 1),), REACH * BS)
        other = lax.dot_general(
            widened,
            col_band,
            (((1,), (1,)), ((), ())),
            precision=lax.Precision.HIGHEST,
            preferred_element_type=jnp.float32,
        )
        return product + other + noise_term

    k_first = tendency(p_cov)
    p_mid = p_cov + time_step * k_first
    k_second = tendency(p_mid)
    return p_cov + 0.5 * time_step * (k_first + k_second)


def split(values):
    high = values.astype(jnp.bfloat16)
    return high, (values - high.astype(jnp.float32)).astype(jnp.bfloat16)


def product(left_high, left_low, right_high, right_low):
    dot = functools.partial(jnp.dot, preferred_element_type=jnp.float32)
    return dot(left_high, right_high) + (dot(left_high, right_low) + dot(left_low, right_high))


def params():
    return pltpu.CompilerParams(vmem_limit_bytes=VMEM_BYTES)


def cost(flops, bytes_accessed):
    return pl.CostEstimate(flops=flops // 64, bytes_accessed=bytes_accessed // 64, transcendentals=0)


def pick_kernel(role, *refs):
    *sources, out = refs
    for index, source in enumerate(sources):

        @pl.when(role[0] == index)
        def _(source=source):
            out[...] = source[...]


def pick(role, *sources):
    shape = sources[0].shape
    block = (1, *shape[1:])

    def spec(index):
        return pl.BlockSpec(block, lambda i, role: (jnp.where(role[0] == index, i, 0), 0, 0, 0))

    return pl.pallas_call(
        pick_kernel,
        grid_spec=pltpu.PrefetchScalarGridSpec(
            num_scalar_prefetch=1,
            grid=(shape[0],),
            in_specs=[spec(index) for index in range(len(sources))],
            out_specs=pl.BlockSpec(block, lambda i, role: (i, 0, 0, 0)),
        ),
        out_shape=jax.ShapeDtypeStruct(shape, sources[0].dtype),
        compiler_params=params(),
        cost_estimate=cost(0, sources[0].size * 8),
    )(role, *sources)


def row_band_kernel(slots, place, blocks, near_high, near_low, far_high, far_low):
    pair = pl.program_id(0)
    for ref in (near_high, near_low, far_high, far_low):
        ref[...] = jnp.zeros_like(ref)
    blocks_dev = HALO // BS
    for half in range(TILE // BS):
        rows = pl.ds(half * BS, BS)
        for slot in range(blocks.shape[1]):
            column = slots[pair * 2 + half, slot]
            at = column - place[0]
            far_at = jnp.where(place[1] == 0, at + blocks_dev, at - blocks_dev)
            is_far = (far_at >= 0) & (far_at < blocks_dev)

            @pl.when((column >= 0) & is_far)
            def _(half=half, slot=slot, far_at=far_at, rows=rows):
                lanes = pl.ds(pl.multiple_of(far_at * BS, BS), BS)
                far_high[0, rows, lanes], far_low[0, rows, lanes] = split(blocks[half, slot])

            @pl.when((column >= 0) & jnp.logical_not(is_far))
            def _(half=half, slot=slot, at=at, rows=rows):
                lanes = pl.ds(pl.multiple_of((at + place[1] * blocks_dev) * BS, BS), BS)
                near_high[0, rows, lanes], near_low[0, rows, lanes] = split(blocks[half, slot])


def row_bands(a_blocks, pattern, place):
    count, slots = pattern.shape
    tiles = count * BS // TILE
    outs = [jax.ShapeDtypeStruct((tiles, TILE, width), jnp.bfloat16) for width in (2 * HALO, HALO)]
    specs = [pl.BlockSpec((1, TILE, width), lambda i, *_: (i, 0, 0)) for width in (2 * HALO, HALO)]
    got = pl.pallas_call(
        row_band_kernel,
        grid_spec=pltpu.PrefetchScalarGridSpec(
            num_scalar_prefetch=2,
            grid=(tiles,),
            in_specs=[pl.BlockSpec((2, slots, BS, BS), lambda i, *_: (i, 0, 0, 0))],
            out_specs=[specs[0], specs[0], specs[1], specs[1]],
        ),
        out_shape=[outs[0], outs[0], outs[1], outs[1]],
        compiler_params=params(),
        cost_estimate=cost(0, a_blocks.size * 4 + tiles * TILE * 3 * HALO * 4),
    )(pattern, place, a_blocks)
    return got[:2], got[2:]


def col_band_kernel(slots, base, core, mine, other, *refs, per_core):
    high, low = refs[-2:]
    step = pl.program_id(0)
    half_rows = slots.shape[0] // 2
    owner = step // per_core
    pair = lax.rem(step, per_core)
    high[...] = jnp.zeros_like(high)
    low[...] = jnp.zeros_like(low)
    for mine_here, blocks in ((True, mine), (False, other)):

        @pl.when((core[0] == owner) == mine_here)
        def _(blocks=blocks):
            for half in range(TILE // BS):
                rows = pl.ds(half * BS, BS)
                for slot in range(blocks.shape[1]):
                    column = slots[owner * half_rows + pair * 2 + half, slot]

                    @pl.when(column >= 0)
                    def _(rows=rows, half=half, slot=slot, column=column):
                        place = column - base[owner] - 2 * pair + REACH
                        lanes = pl.ds(pl.multiple_of(place * BS, BS), BS)
                        high[0, rows, lanes], low[0, rows, lanes] = split(blocks[half, slot])


def col_bands(mine, other, slots, base, core, chunk, into):
    count, width = slots.shape
    per_core = count * BS // TILE // 2
    tiles = 2 * per_core * CHUNKS
    out = jax.ShapeDtypeStruct((tiles, TILE, WIDE), jnp.bfloat16)

    def tile(i, *_):
        return (i // per_core * (tiles // 2) + chunk * per_core + lax.rem(i, per_core), 0, 0)

    blocks = pl.BlockSpec((2, width, BS, BS), lambda i, *_: (lax.rem(i, per_core), 0, 0, 0))
    spec = pl.BlockSpec((1, TILE, WIDE), tile)
    return pl.pallas_call(
        functools.partial(col_band_kernel, per_core=per_core),
        grid_spec=pltpu.PrefetchScalarGridSpec(
            num_scalar_prefetch=3,
            grid=(2 * per_core,),
            in_specs=[blocks, blocks] + [pl.BlockSpec(memory_space=pl.ANY)] * len(into),
            out_specs=[spec, spec],
        ),
        out_shape=[out, out],
        input_output_aliases={5: 0, 6: 1} if into else {},
        compiler_params=params(),
        cost_estimate=cost(0, mine.size * 16 + tiles * TILE * WIDE * 4),
    )(slots, base, core, mine, other, *into)


def resident(array):
    return pl.BlockSpec(array.shape, lambda *_: (0,) * array.ndim, pipeline_mode=pl.Buffered(1))


def near_kernel(core, band_high, band_low, own, sibling, *refs, scale):
    *bases, out, ext_high, ext_low = refs
    rows = own.shape[0]
    part = rows // max(len(bases), 1)

    def place(own_at, sibling_at):
        for at, ref in ((own_at, own), (sibling_at, sibling)):
            ext_high[pl.ds(at, rows), :], ext_low[pl.ds(at, rows), :] = split(ref[...])

    def multiply(tile, reach):
        got = product(
            band_high[tile, :, reach],
            band_low[tile, :, reach],
            ext_high[reach, :],
            ext_low[reach, :],
        )
        got = scale * got
        at = tile * TILE
        if bases:
            got += bases[at // part][pl.ds(at % part, TILE), :]
        out[pl.ds(at, TILE), :] = got

    @pl.when(core[0] == 0)
    def _():
        place(0, rows)
        for tile in range(rows // TILE):
            multiply(tile, slice(0, HALO + (tile + 1) * TILE))

    @pl.when(core[0] == 1)
    def _():
        place(rows, 0)
        for tile in range(rows // TILE):
            multiply(tile, slice(tile * TILE, HALO + rows))


def near(core, bands, own, sibling, scale, bases=(), place=0, lanes=512):
    rows, cols = own.shape
    start = place // lanes
    spec = pl.BlockSpec((rows, lanes), lambda i, *_: (0, i))
    base = pl.BlockSpec((rows // max(len(bases), 1), lanes), lambda i, *_: (0, i + start))
    return pl.pallas_call(
        functools.partial(near_kernel, scale=scale),
        grid_spec=pltpu.PrefetchScalarGridSpec(
            num_scalar_prefetch=1,
            grid=(cols // lanes,),
            in_specs=[resident(bands[0]), resident(bands[1]), spec, spec] + [base] * len(bases),
            out_specs=spec,
            scratch_shapes=[pltpu.VMEM((2 * rows, lanes), jnp.bfloat16)] * 2,
        ),
        out_shape=jax.ShapeDtypeStruct((rows, cols), jnp.float32),
        compiler_params=params(),
        cost_estimate=cost(6 * rows * cols * 1664, 3 * rows * cols * 4),
    )(core, *bands, own, sibling, *bases)


def diagonal(noise, shape, row_at, col_at):
    row = lax.broadcasted_iota(jnp.int32, shape, 0) + row_at
    col = lax.broadcasted_iota(jnp.int32, shape, 1) + col_at
    return jnp.where(row == col, noise, 0.0)


def far_kernel(where, band_high, band_low, far, relayed, noise, *refs, scale, add_noise):
    *bases, out, far_high, far_low = refs
    rows, lanes = far.shape
    part = rows // len(bases)

    @pl.when(where[2] == 0)
    def _():
        far_high[...], far_low[...] = split(far[...])

    @pl.when(where[2] == 1)
    def _():
        far_high[...], far_low[...] = split(relayed[...])

    def multiply(tile, reach):
        got = product(
            band_high[tile, :, reach],
            band_low[tile, :, reach],
            far_high[reach, :],
            far_low[reach, :],
        )
        at = tile * TILE
        base = bases[at // part][pl.ds(at % part, TILE), :]
        out[pl.ds(at, TILE), :] = base + scale * got

    @pl.when(where[0] == 0)
    def _():
        for tile in range(rows // TILE):
            multiply(tile, slice(tile * TILE, rows))

    @pl.when(where[0] == 1)
    def _():
        for tile in range(rows // TILE):
            multiply(tile, slice(0, (tile + 1) * TILE))

    if add_noise:
        shift = where[1] + pl.program_id(0) * lanes

        @pl.when((shift < rows) & (shift + lanes > 0))
        def _():
            for tile in range(rows // TILE):
                span = pl.ds(tile * TILE, TILE)
                out[span, :] += time_step * diagonal(noise[span, :], (TILE, lanes), tile * TILE, shift)


def far_part(where, bands, far, noise, bases, place, scale, add_noise, in_place=False, lanes=256):
    straight, relayed = far
    rows, cols = straight.shape
    start = place // lanes
    base = pl.BlockSpec((rows // len(bases), lanes), lambda i, *_: (0, i + start))
    out = base if in_place else pl.BlockSpec((rows, lanes), lambda i, *_: (0, i))

    def source(relay):
        return pl.BlockSpec((rows, lanes), lambda i, where: (0, jnp.where(where[2] == relay, i, 0)))

    return pl.pallas_call(
        functools.partial(far_kernel, scale=scale, add_noise=add_noise),
        grid_spec=pltpu.PrefetchScalarGridSpec(
            num_scalar_prefetch=1,
            grid=(cols // lanes,),
            in_specs=[resident(bands[0]), resident(bands[1]), source(0), source(1), resident(noise)]
            + [base] * len(bases),
            out_specs=out,
            scratch_shapes=[pltpu.VMEM((rows, lanes), jnp.bfloat16)] * 2,
        ),
        out_shape=jax.ShapeDtypeStruct(bases[0].shape if in_place else (rows, cols), jnp.float32),
        input_output_aliases={6: 0} if in_place else {},
        compiler_params=params(),
        cost_estimate=cost(6 * rows * cols * 640, 3 * rows * cols * 4),
    )(where, *bands, straight, relayed, noise, *bases)


def right_product(bands, pieces, ext_high, ext_low):
    step = pl.program_id(0)

    @pl.when(step == 0)
    def _():
        at = 0
        for piece in pieces:
            span = pl.ds(at, piece.shape[1])
            ext_high[:, span], ext_low[:, span] = split(piece[...])
            at += piece.shape[1]

    dot = functools.partial(
        lax.dot_general,
        dimension_numbers=(((1,), (1,)), ((), ())),
        preferred_element_type=jnp.float32,
    )
    reach = pl.ds(pl.multiple_of(step * TILE, TILE), WIDE)
    high, low = ext_high[:, reach], ext_low[:, reach]
    band_high, band_low = bands
    return dot(high, band_high) + (dot(high, band_low) + dot(low, band_high))


def right_first_kernel(where, *refs, half_cols):
    high, low, low_side, own, high_side, p_tile, m_low, m_high, noise = refs[:9]
    w_low, w_high, base, ext_high, ext_low = refs[9:]
    step = pl.program_id(0)
    rows, lanes = p_tile.shape
    v = time_step * right_product((high[0], low[0]), (low_side, own, high_side), ext_high, ext_low)
    shift = where[1] + step * lanes
    for here, m_tile, w in ((0, m_low, w_low), (1, m_high, w_high)):

        @pl.when(step // half_cols == here)
        def _(m_tile=m_tile, w=w):
            base[...] = p_tile[...] + (m_tile[...] + v)
            w[...] = m_tile[...] + 0.5 * v

            @pl.when((shift < rows) & (shift + lanes > 0))
            def _():
                w[...] -= (0.5 * time_step) * diagonal(noise[...], (rows, lanes), 0, shift)


def right_specs(rows, part, half_cols):
    def whole(width):
        return pl.BlockSpec((rows, width), lambda i, *_: (part, 0), pipeline_mode=pl.Buffered(1))

    full = pl.BlockSpec((rows, TILE), lambda i, *_: (part, i))
    first = pl.BlockSpec((rows, TILE), lambda i, *_: (part, jnp.minimum(i, half_cols - 1)))
    second = pl.BlockSpec((rows, TILE), lambda i, *_: (part, jnp.maximum(i - half_cols, 0)))
    return whole, full, first, second


BAND = pl.BlockSpec((1, TILE, WIDE), lambda i, *_: (i, 0, 0))


def right_first(where, bands, p, sides, m, noise, part, parts):
    rows, cols = p.shape
    rows //= parts
    half_cols = cols // TILE // 2
    whole, full, first, second = right_specs(rows, part, half_cols)
    _, out_full, out_first, out_second = right_specs(rows, 0, half_cols)
    half = jax.ShapeDtypeStruct((rows, cols // 2), jnp.float32)
    return pl.pallas_call(
        functools.partial(right_first_kernel, half_cols=half_cols),
        grid_spec=pltpu.PrefetchScalarGridSpec(
            num_scalar_prefetch=1,
            grid=(cols // TILE,),
            in_specs=[BAND, BAND, whole(HALO), whole(cols), whole(HALO), full]
            + [first, second, whole(1)],
            out_specs=[out_first, out_second, out_full],
            scratch_shapes=[pltpu.VMEM((rows, cols + 2 * HALO), jnp.bfloat16)] * 2,
        ),
        out_shape=[half, half, jax.ShapeDtypeStruct((rows, cols), jnp.float32)],
        compiler_params=params(),
        cost_estimate=cost(6 * rows * cols * WIDE, 5 * rows * cols * 4),
    )(where, *bands, sides[0], p, sides[1], p, *m, noise)


def right_last_kernel(high, low, low_side, w_low, w_high, high_side, g_low, g_high, *refs, half_cols):
    out, ext_high, ext_low = refs[-3:]
    pieces = (low_side, w_low, w_high, high_side)
    got = time_step * right_product((high[0], low[0]), pieces, ext_high, ext_low)
    for here, g in ((0, g_low), (1, g_high)):

        @pl.when(pl.program_id(0) // half_cols == here)
        def _(g=g):
            out[...] = g[...] + got


def right_last(bands, w, sides, g, into, part, parts):
    rows, half = w[0].shape
    half_cols = half // TILE
    whole, _, _, _ = right_specs(rows, 0, half_cols)
    _, full, first, second = right_specs(rows, part, half_cols)
    prior = [] if into is None else [into]
    return pl.pallas_call(
        functools.partial(right_last_kernel, half_cols=half_cols),
        grid=(2 * half_cols,),
        in_specs=[BAND, BAND, whole(HALO), whole(half), whole(half), whole(HALO), first, second]
        + [pl.BlockSpec(memory_space=pl.ANY)] * len(prior),
        out_specs=full,
        scratch_shapes=[pltpu.VMEM((rows, 2 * (half + HALO)), jnp.bfloat16)] * 2,
        out_shape=jax.ShapeDtypeStruct((rows * parts, 2 * half), jnp.float32),
        input_output_aliases={8: 0} if prior else {},
        compiler_params=params(),
        cost_estimate=cost(6 * rows * 2 * half * WIDE, 5 * rows * 2 * half * 4),
    )(*bands, sides[0], *w, sides[1], *g, *prior)


def permute(array, moves):
    return lax.ppermute(array, "row", moves)


def permute_by_column(array, moves):
    cols = lax.axis_size("col")
    pairs = [
        (source * cols + col, target * cols + col)
        for col in range(cols)
        for source, target in moves(col)
    ]
    return lax.ppermute(array, ("row", "col"), pairs)


def dev(chip, core):
    return 2 * chip + core


def after(value, *others):
    return lax.optimization_barrier((value, *others))[0]


def off_chip_rows(x):
    count = lax.axis_size("row")
    moves = []
    for low in range(1, count - 1, 2):
        moves += [(low, low + 1), (low + 1, low)]
    straight = [pair for pair in moves if set(pair) != {dev(1, 1), dev(2, 0)}]
    first = permute(x[0], moves)
    hop = permute(x[1], [(dev(1, 1), dev(3, 1)), (dev(2, 0), dev(0, 0))])
    second = permute(x[1], straight)
    return first, second, hop


def relay(hop):
    return permute(hop, [(dev(3, 1), dev(2, 0)), (dev(0, 0), dev(1, 1))])


def sides(low_half, high_half):
    cols = lax.axis_size("col")
    low_side = lax.ppermute(high_half, "col", [(i, i + 1) for i in range(cols - 1)])
    high_side = lax.ppermute(low_half, "col", [(i + 1, i) for i in range(cols - 1)])
    return low_side, high_side


def halves(x):
    middle = x.shape[1] // 2
    return lax.slice_in_dim(x, 0, middle, axis=1), lax.slice_in_dim(x, middle, None, axis=1)


def paired_body(p_cov, a_blocks, pattern, q_diag):
    rows_dev, cols_dev = p_cov.shape
    row = lax.axis_index("row")
    col = lax.axis_index("col")
    chip = row // 2
    at_core = lax.rem(row, 2)
    core = jnp.full((1,), at_core, jnp.int32)
    relayed = ((row == dev(1, 1)) | (row == dev(2, 0))).astype(jnp.int32)
    offset = col * cols_dev - row * rows_dev
    where = [
        jnp.stack([at_core, offset + half * HALO, relayed * half]).astype(jnp.int32)
        for half in (0, 1)
    ]
    count = lax.axis_size("row")
    swap = [(i, i ^ 1) for i in range(count)]
    noise = q_diag.reshape(rows_dev, 1)
    col_count = cols_dev // BS

    all_slots = lax.all_gather(pattern, "row", axis=0, tiled=True)
    place = jnp.stack([row * (rows_dev // BS), at_core]).astype(jnp.int32)
    near_bands, far_bands = row_bands(a_blocks, pattern, place)

    p_sent = after(p_cov, all_slots)
    sibling = permute(p_sent, swap)
    p = halves(p_sent)
    first, straight, hop = off_chip_rows(p)
    p_far = ((first, first), (straight, relay(hop)))
    p_sides = sides(*p)
    m_near = near(core, near_bands, p_cov, sibling, time_step)

    def far_of_p(h, far):
        return far_part(where[h], far_bands, far, noise, [m_near], h * HALO, time_step, True)

    away = chip ^ col
    by_core = jnp.array([[0, 1, 2, 3], [0, 4, 1, 3]], jnp.int32)
    role = by_core[at_core, away].reshape(1)
    size = a_blocks.shape[0] // CHUNKS
    owns = [lax.slice_in_dim(a_blocks, k * size, (k + 1) * size, axis=0) for k in range(CHUNKS)]
    owns = [after(own, all_slots) for own in owns]
    ones = [
        permute_by_column(own, lambda c: [(dev(c, 0), dev(c ^ 1, 0)), (dev(c, 1), dev(c ^ 2, 1))])
        for own in owns
    ]
    twos = [permute_by_column(own, lambda c: [(dev(c, 0), dev(c ^ 2, 0))]) for own in owns]
    ones = [after(ones[0], sibling), after(ones[1], m_near)]
    seconds = [
        permute_by_column(
            one, lambda c: [(dev(c ^ 1, 0), dev(c ^ 3, 0)), (dev(c ^ 2, 1), dev(c ^ 3, 1))]
        )
        for one in ones
    ]
    thirds = [
        permute_by_column(second, lambda c: [(dev(c ^ 3, 1), dev(c ^ 1, 1))])
        for second in (after(seconds[0], m_near), seconds[1])
    ]
    p_far = [
        [after(part, *held) for part in parts]
        for parts, held in zip(p_far, (seconds[:1], (thirds[0], *twos, *p_sides)))
    ]
    m = [far_of_p(h, p_far[h]) for h in (0, 1)]
    m_sibling = [permute(part, swap) for part in m]
    m_first, m_second, m_hop = off_chip_rows(m)
    half_step = 0.5 * time_step

    forced_mine = ((m[0],), (m[1],))
    mines, others = [], []
    for chunk in range(CHUNKS):
        own = after(owns[chunk], *forced_mine[chunk])
        mines.append(pick(role, own, ones[chunk], twos[chunk], seconds[chunk], thirds[chunk]))
        others.append(permute(mines[chunk], swap))
    bands = ()
    for chunk in range(CHUNKS):
        first_rows = [col * col_count + half * (col_count // 2) + chunk * size for half in (0, 1)]
        slots = jnp.concatenate(
            [lax.dynamic_slice_in_dim(all_slots, row_at, size, axis=0) for row_at in first_rows], axis=0
        )
        base = jnp.stack(first_rows).astype(jnp.int32)
        bands = col_bands(mines[chunk], others[chunk], slots, base, core, chunk, bands)

    parts = 2
    got = []
    for part in range(parts):
        shift = where[0] - jnp.array([0, part * (rows_dev // parts), 0], jnp.int32)
        noise_then = after(noise, m_sibling[1]) if part else noise
        got.append(right_first(shift, bands, p_cov, p_sides, m, noise_then, part, parts))
    w_sides = [sides(w_low, w_high) for w_low, w_high, _ in got]
    bases = [base for _, _, base in got]
    m_landed = relay(after(m_hop, bases[0]))
    g = [near(core, near_bands, m[h], m_sibling[h], half_step, bases, h * HALO) for h in (0, 1)]
    g[0] = far_part(where[0], far_bands, (m_first, m_first), noise, [g[0]], 0, half_step, False)
    out = None
    for part in range(parts):
        out = right_last(bands, got[part][:2], w_sides[part], g, out, part, parts)
    return far_part(where[1], far_bands, (m_second, m_landed), noise, [out], HALO, half_step, False, True)


def solution(mesh):
    def body(p_cov, a_blocks, pattern, q_diag):
        rows_dev, cols_dev = p_cov.shape
        rows, cols = lax.axis_size("row"), lax.axis_size("col")
        paired = rows == 8 and cols == 4 and rows_dev == HALO and cols_dev == 2 * HALO
        return (paired_body if paired else general_body)(p_cov, a_blocks, pattern, q_diag)

    return jax.shard_map(
        body,
        mesh=mesh,
        in_specs=(P("row", "col"), P("row", None, None, None), P("row", None), P("row")),
        out_specs=P("row", "col"),
        check_vma=False,
    )
```

```python
import functools

import jax
import jax.numpy as jnp
from jax import lax
from jax.experimental import pallas as pl
from jax.experimental.pallas import tpu as pltpu
from jax.sharding import PartitionSpec as P

BS = 128
REACH = 8
HALO = REACH * BS
TILE = 2 * BS
WIDE = TILE + 2 * HALO
CHUNKS = 2

time_step = 0.25

VMEM_BYTES = 56 * 1024 * 1024


def shifted(array, axis, by):
    peers = lax.axis_size(axis)
    pairs = [(i, i + by) for i in range(peers) if 0 <= i + by < peers]
    return lax.ppermute(array, axis, pairs)


def broadcast(value, axis, source):
    kept = jnp.where(lax.axis_index(axis) == source, value, 0).astype(value.dtype)
    return lax.psum(kept, axis)


def with_halo(block, sides, width):
    for axis, dim in sides:
        count = lax.axis_size(axis)
        forward = [(i, i + 1) for i in range(count - 1)]
        backward = [(target, source) for source, target in forward]
        low = lax.ppermute(
            lax.slice_in_dim(block, block.shape[dim] - width, None, axis=dim), axis, forward
        )
        high = lax.ppermute(lax.slice_in_dim(block, 0, width, axis=dim), axis, backward)
        block = jnp.concatenate([low, block, high], axis=dim)
    return block


def band_matrix(blocks, slots, first_block, extent):
    picks = jnp.arange(extent, dtype=jnp.int32)[None, None, :]
    onehot = ((slots - first_block)[:, :, None] == picks).astype(jnp.float32)
    banded = jnp.einsum("bse,bsxy->bxey", onehot, blocks, precision=lax.Precision.HIGHEST)
    return banded.reshape(blocks.shape[0] * BS, extent * BS)


def general_body(p_cov, a_blocks, pattern, q_diag):
    rows_dev, cols_dev = p_cov.shape
    row_count = lax.axis_size("row")
    col_count = lax.axis_size("col")
    row_idx = lax.axis_index("row")
    col_idx = lax.axis_index("col")
    row_blocks = rows_dev // BS
    span_devs = REACH * BS // rows_dev
    group_rows = row_count // col_count
    global_rows = row_idx * rows_dev + jnp.arange(rows_dev, dtype=jnp.int32)[:, None]
    global_cols = col_idx * cols_dev + jnp.arange(cols_dev, dtype=jnp.int32)[None, :]
    noise_term = jnp.where(global_rows == global_cols, q_diag[:, None], 0.0)
    row_band = band_matrix(
        a_blocks,
        pattern,
        row_idx * row_blocks - span_devs * row_blocks,
        (2 * span_devs + 1) * row_blocks,
    )

    def forward(p_local):
        pieces = []
        for offset in range(-span_devs, span_devs + 1):
            if offset == 0:
                pieces.append(p_local)
            else:
                pieces.append(shifted(p_local, "row", -offset))
        extended = jnp.concatenate(pieces, axis=0)
        return jnp.dot(
            row_band, extended, precision=lax.Precision.HIGHEST, preferred_element_type=jnp.float32
        )

    fetched_blocks = []
    fetched_slots = []
    for member in range(group_rows):
        got_blocks, got_slots = (
            broadcast(a_blocks, "row", col_idx * group_rows + member),
            broadcast(pattern.astype(jnp.float32), "row", col_idx * group_rows + member),
        )
        fetched_blocks.append(got_blocks)
        fetched_slots.append(got_slots)
    col_blocks = jnp.concatenate(fetched_blocks, axis=0)
    col_slots = jnp.concatenate(fetched_slots, axis=0).astype(jnp.int32)
    col_band = band_matrix(
        col_blocks, col_slots, col_idx * (cols_dev // BS) - REACH, cols_dev // BS + 2 * REACH
    )

    def tendency(p_local):
        product = forward(p_local)
        widened = with_halo(p_local, (("col", 1),), REACH * BS)
        other = lax.dot_general(
            widened,
            col_band,
            (((1,), (1,)), ((), ())),
            precision=lax.Precision.HIGHEST,
            preferred_element_type=jnp.float32,
        )
        return product + other + noise_term

    k_first = tendency(p_cov)
    p_mid = p_cov + time_step * k_first
    k_second = tendency(p_mid)
    return p_cov + 0.5 * time_step * (k_first + k_second)


def split(values):
    high = values.astype(jnp.bfloat16)
    return high, (values - high.astype(jnp.float32)).astype(jnp.bfloat16)


def product(left_high, left_low, right_high, right_low):
    dot = functools.partial(jnp.dot, preferred_element_type=jnp.float32)
    return dot(left_high, right_high) + (dot(left_high, right_low) + dot(left_low, right_high))


def params():
    return pltpu.CompilerParams(vmem_limit_bytes=VMEM_BYTES)


def cost(flops, bytes_accessed):
    return pl.CostEstimate(flops=flops // 64, bytes_accessed=bytes_accessed // 64, transcendentals=0)


def pick_kernel(role, *refs):
    *sources, out = refs
    for index, source in enumerate(sources):

        @pl.when(role[0] == index)
        def _(source=source):
            out[...] = source[...]


def pick(role, *sources):
    shape = sources[0].shape
    block = (1, *shape[1:])

    def spec(index):
        return pl.BlockSpec(block, lambda i, role: (jnp.where(role[0] == index, i, 0), 0, 0, 0))

    return pl.pallas_call(
        pick_kernel,
        grid_spec=pltpu.PrefetchScalarGridSpec(
            num_scalar_prefetch=1,
            grid=(shape[0],),
            in_specs=[spec(index) for index in range(len(sources))],
            out_specs=pl.BlockSpec(block, lambda i, role: (i, 0, 0, 0)),
        ),
        out_shape=jax.ShapeDtypeStruct(shape, sources[0].dtype),
        compiler_params=params(),
        cost_estimate=cost(0, sources[0].size * 8),
    )(role, *sources)


def row_band_kernel(slots, place, blocks, near_high, near_low, far_high, far_low):
    pair = pl.program_id(0)
    for ref in (near_high, near_low, far_high, far_low):
        ref[...] = jnp.zeros_like(ref)
    blocks_dev = HALO // BS
    for half in range(TILE // BS):
        rows = pl.ds(half * BS, BS)
        for slot in range(blocks.shape[1]):
            column = slots[pair * 2 + half, slot]
            at = column - place[0]
            far_at = jnp.where(place[1] == 0, at + blocks_dev, at - blocks_dev)
            is_far = (far_at >= 0) & (far_at < blocks_dev)

            @pl.when((column >= 0) & is_far)
            def _(half=half, slot=slot, far_at=far_at, rows=rows):
                lanes = pl.ds(pl.multiple_of(far_at * BS, BS), BS)
                far_high[0, rows, lanes], far_low[0, rows, lanes] = split(blocks[half, slot])

            @pl.when((column >= 0) & jnp.logical_not(is_far))
            def _(half=half, slot=slot, at=at, rows=rows):
                lanes = pl.ds(pl.multiple_of((at + place[1] * blocks_dev) * BS, BS), BS)
                near_high[0, rows, lanes], near_low[0, rows, lanes] = split(blocks[half, slot])


def row_bands(a_blocks, pattern, place):
    count, slots = pattern.shape
    tiles = count * BS // TILE
    outs = [jax.ShapeDtypeStruct((tiles, TILE, width), jnp.bfloat16) for width in (2 * HALO, HALO)]
    specs = [pl.BlockSpec((1, TILE, width), lambda i, *_: (i, 0, 0)) for width in (2 * HALO, HALO)]
    got = pl.pallas_call(
        row_band_kernel,
        grid_spec=pltpu.PrefetchScalarGridSpec(
            num_scalar_prefetch=2,
            grid=(tiles,),
            in_specs=[pl.BlockSpec((2, slots, BS, BS), lambda i, *_: (i, 0, 0, 0))],
            out_specs=[specs[0], specs[0], specs[1], specs[1]],
        ),
        out_shape=[outs[0], outs[0], outs[1], outs[1]],
        compiler_params=params(),
        cost_estimate=cost(0, a_blocks.size * 4 + tiles * TILE * 3 * HALO * 4),
    )(pattern, place, a_blocks)
    return got[:2], got[2:]


def col_band_kernel(slots, base, core, mine, other, *refs, per_core):
    high, low = refs[-2:]
    step = pl.program_id(0)
    half_rows = slots.shape[0] // 2
    owner = step // per_core
    pair = lax.rem(step, per_core)
    high[...] = jnp.zeros_like(high)
    low[...] = jnp.zeros_like(low)
    for mine_here, blocks in ((True, mine), (False, other)):

        @pl.when((core[0] == owner) == mine_here)
        def _(blocks=blocks):
            for half in range(TILE // BS):
                rows = pl.ds(half * BS, BS)
                for slot in range(blocks.shape[1]):
                    column = slots[owner * half_rows + pair * 2 + half, slot]

                    @pl.when(column >= 0)
                    def _(rows=rows, half=half, slot=slot, column=column):
                        place = column - base[owner] - 2 * pair + REACH
                        lanes = pl.ds(pl.multiple_of(place * BS, BS), BS)
                        high[0, rows, lanes], low[0, rows, lanes] = split(blocks[half, slot])


def col_bands(mine, other, slots, base, core, chunk, into):
    count, width = slots.shape
    per_core = count * BS // TILE // 2
    tiles = 2 * per_core * CHUNKS
    out = jax.ShapeDtypeStruct((tiles, TILE, WIDE), jnp.bfloat16)

    def tile(i, *_):
        return (i // per_core * (tiles // 2) + chunk * per_core + lax.rem(i, per_core), 0, 0)

    def source(first_on):
        def place(i, slots, base, core):
            first = jnp.minimum(i, per_core - 1)
            return (jnp.where(core[0] == first_on, first, jnp.maximum(i - per_core, 0)), 0, 0, 0)

        return pl.BlockSpec((2, width, BS, BS), place)

    spec = pl.BlockSpec((1, TILE, WIDE), tile)
    return pl.pallas_call(
        functools.partial(col_band_kernel, per_core=per_core),
        grid_spec=pltpu.PrefetchScalarGridSpec(
            num_scalar_prefetch=3,
            grid=(2 * per_core,),
            in_specs=[source(0), source(1)] + [pl.BlockSpec(memory_space=pl.ANY)] * len(into),
            out_specs=[spec, spec],
        ),
        out_shape=[out, out],
        input_output_aliases={5: 0, 6: 1} if into else {},
        compiler_params=params(),
        cost_estimate=cost(0, mine.size * 16 + tiles * TILE * WIDE * 4),
    )(slots, base, core, mine, other, *into)


def resident(array):
    return pl.BlockSpec(array.shape, lambda *_: (0,) * array.ndim, pipeline_mode=pl.Buffered(1))


def near_kernel(core, band_high, band_low, *refs, scale, pieces):
    owns, siblings = refs[:pieces], refs[pieces : 2 * pieces]
    *bases, out, ext_high, ext_low = refs[2 * pieces :]
    rows = owns[0].shape[0]
    piece = pl.program_id(0) // (pl.num_programs(0) // pieces)
    part = rows // max(len(bases), 1)

    def place(own_at, sibling_at):
        for here in range(pieces):

            @pl.when(piece == here)
            def _(here=here):
                for at, ref in ((own_at, owns[here]), (sibling_at, siblings[here])):
                    ext_high[pl.ds(at, rows), :], ext_low[pl.ds(at, rows), :] = split(ref[...])

    def multiply(tile, reach):
        got = product(
            band_high[tile, :, reach],
            band_low[tile, :, reach],
            ext_high[reach, :],
            ext_low[reach, :],
        )
        got = scale * got
        at = tile * TILE
        if bases:
            got += bases[at // part][pl.ds(at % part, TILE), :]
        out[pl.ds(at, TILE), :] = got

    @pl.when(core[0] == 0)
    def _():
        place(0, rows)
        for tile in range(rows // TILE):
            multiply(tile, slice(0, HALO + (tile + 1) * TILE))

    @pl.when(core[0] == 1)
    def _():
        place(rows, 0)
        for tile in range(rows // TILE):
            multiply(tile, slice(tile * TILE, HALO + rows))


def near(core, bands, owns, siblings, scale, bases=(), lanes=512):
    rows = owns[0].shape[0]
    pieces = len(owns)
    steps = owns[0].shape[1] // lanes
    cols = pieces * steps * lanes

    def piece(index):
        return pl.BlockSpec(
            (rows, lanes), lambda i, *_: (0, jnp.clip(i - index * steps, 0, steps - 1))
        )

    base = pl.BlockSpec((rows // max(len(bases), 1), lanes), lambda i, *_: (0, i))
    return pl.pallas_call(
        functools.partial(near_kernel, scale=scale, pieces=pieces),
        grid_spec=pltpu.PrefetchScalarGridSpec(
            num_scalar_prefetch=1,
            grid=(pieces * steps,),
            in_specs=[resident(bands[0]), resident(bands[1])]
            + [piece(index) for index in range(pieces)] * 2
            + [base] * len(bases),
            out_specs=pl.BlockSpec((rows, lanes), lambda i, *_: (0, i)),
            scratch_shapes=[pltpu.VMEM((2 * rows, lanes), jnp.bfloat16)] * 2,
        ),
        out_shape=jax.ShapeDtypeStruct((rows, cols), jnp.float32),
        compiler_params=params(),
        cost_estimate=cost(6 * rows * cols * 1664, 3 * rows * cols * 4),
    )(core, *bands, *owns, *siblings, *bases)


def diagonal(noise, shape, row_at, col_at):
    row = lax.broadcasted_iota(jnp.int32, shape, 0) + row_at
    col = lax.broadcasted_iota(jnp.int32, shape, 1) + col_at
    return jnp.where(row == col, noise, 0.0)


def far_kernel(where, band_high, band_low, far, relayed, noise, *refs, scale, add_noise):
    *bases, out, far_high, far_low = refs
    rows, lanes = far.shape
    part = rows // len(bases)

    @pl.when(where[2] == 0)
    def _():
        far_high[...], far_low[...] = split(far[...])

    @pl.when(where[2] == 1)
    def _():
        far_high[...], far_low[...] = split(relayed[...])

    def multiply(tile, reach):
        got = product(
            band_high[tile, :, reach],
            band_low[tile, :, reach],
            far_high[reach, :],
            far_low[reach, :],
        )
        at = tile * TILE
        base = bases[at // part][pl.ds(at % part, TILE), :]
        out[pl.ds(at, TILE), :] = base + scale * got

    @pl.when(where[0] == 0)
    def _():
        for tile in range(rows // TILE):
            multiply(tile, slice(tile * TILE, rows))

    @pl.when(where[0] == 1)
    def _():
        for tile in range(rows // TILE):
            multiply(tile, slice(0, (tile + 1) * TILE))

    if add_noise:
        shift = where[1] + pl.program_id(0) * lanes

        @pl.when((shift < rows) & (shift + lanes > 0))
        def _():
            for tile in range(rows // TILE):
                span = pl.ds(tile * TILE, TILE)
                out[span, :] += time_step * diagonal(noise[span, :], (TILE, lanes), tile * TILE, shift)


def far_part(where, bands, far, noise, bases, place, scale, add_noise, in_place=False, lanes=256):
    straight, relayed = far
    rows, cols = straight.shape
    start = place // lanes
    base = pl.BlockSpec((rows // len(bases), lanes), lambda i, *_: (0, i + start))
    out = base if in_place else pl.BlockSpec((rows, lanes), lambda i, *_: (0, i))

    def source(relay):
        return pl.BlockSpec((rows, lanes), lambda i, where: (0, jnp.where(where[2] == relay, i, 0)))

    return pl.pallas_call(
        functools.partial(far_kernel, scale=scale, add_noise=add_noise),
        grid_spec=pltpu.PrefetchScalarGridSpec(
            num_scalar_prefetch=1,
            grid=(cols // lanes,),
            in_specs=[resident(bands[0]), resident(bands[1]), source(0), source(1), resident(noise)]
            + [base] * len(bases),
            out_specs=out,
            scratch_shapes=[pltpu.VMEM((rows, lanes), jnp.bfloat16)] * 2,
        ),
        out_shape=jax.ShapeDtypeStruct(bases[0].shape if in_place else (rows, cols), jnp.float32),
        input_output_aliases={6: 0} if in_place else {},
        compiler_params=params(),
        cost_estimate=cost(6 * rows * cols * 640, 3 * rows * cols * 4),
    )(where, *bands, straight, relayed, noise, *bases)


def right_product(bands, pieces, ext_high, ext_low):
    step = pl.program_id(0)

    @pl.when(step == 0)
    def _():
        at = 0
        for piece in pieces:
            span = pl.ds(at, piece.shape[1])
            ext_high[:, span], ext_low[:, span] = split(piece[...])
            at += piece.shape[1]

    dot = functools.partial(
        lax.dot_general,
        dimension_numbers=(((1,), (1,)), ((), ())),
        preferred_element_type=jnp.float32,
    )
    reach = pl.ds(pl.multiple_of(step * TILE, TILE), WIDE)
    high, low = ext_high[:, reach], ext_low[:, reach]
    band_high, band_low = bands
    return dot(high, band_high) + (dot(high, band_low) + dot(low, band_high))


def right_first_kernel(where, *refs, half_cols):
    high, low, low_side, own, high_side, p_tile, m_low, m_high, noise = refs[:9]
    w_low, w_high, base, ext_high, ext_low = refs[9:]
    step = pl.program_id(0)
    rows, lanes = p_tile.shape
    v = time_step * right_product((high[0], low[0]), (low_side, own, high_side), ext_high, ext_low)
    shift = where[1] + step * lanes
    for here, m_tile, w in ((0, m_low, w_low), (1, m_high, w_high)):

        @pl.when(step // half_cols == here)
        def _(m_tile=m_tile, w=w):
            base[...] = p_tile[...] + (m_tile[...] + v)
            w[...] = m_tile[...] + 0.5 * v

            @pl.when((shift < rows) & (shift + lanes > 0))
            def _():
                w[...] -= (0.5 * time_step) * diagonal(noise[...], (rows, lanes), 0, shift)


def right_specs(rows, part, half_cols):
    def whole(width):
        return pl.BlockSpec((rows, width), lambda i, *_: (part, 0), pipeline_mode=pl.Buffered(1))

    full = pl.BlockSpec((rows, TILE), lambda i, *_: (part, i))
    first = pl.BlockSpec((rows, TILE), lambda i, *_: (part, jnp.minimum(i, half_cols - 1)))
    second = pl.BlockSpec((rows, TILE), lambda i, *_: (part, jnp.maximum(i - half_cols, 0)))
    return whole, full, first, second


BAND = pl.BlockSpec((1, TILE, WIDE), lambda i, *_: (i, 0, 0))


def right_first(where, bands, p, sides, m, noise, part, parts):
    rows, cols = p.shape
    rows //= parts
    half_cols = cols // TILE // 2
    whole, full, first, second = right_specs(rows, part, half_cols)
    _, out_full, out_first, out_second = right_specs(rows, 0, half_cols)
    half = jax.ShapeDtypeStruct((rows, cols // 2), jnp.float32)
    return pl.pallas_call(
        functools.partial(right_first_kernel, half_cols=half_cols),
        grid_spec=pltpu.PrefetchScalarGridSpec(
            num_scalar_prefetch=1,
            grid=(cols // TILE,),
            in_specs=[BAND, BAND, whole(HALO), whole(cols), whole(HALO), full]
            + [first, second, whole(1)],
            out_specs=[out_first, out_second, out_full],
            scratch_shapes=[pltpu.VMEM((rows, cols + 2 * HALO), jnp.bfloat16)] * 2,
        ),
        out_shape=[half, half, jax.ShapeDtypeStruct((rows, cols), jnp.float32)],
        compiler_params=params(),
        cost_estimate=cost(6 * rows * cols * WIDE, 5 * rows * cols * 4),
    )(where, *bands, sides[0], p, sides[1], p, *m, noise)


def right_last_kernel(high, low, low_side, w_low, w_high, high_side, g, *refs):
    out, ext_high, ext_low = refs[-3:]
    pieces = (low_side, w_low, w_high, high_side)
    got = time_step * right_product((high[0], low[0]), pieces, ext_high, ext_low)
    out[...] = g[...] + got


def right_last(bands, w, sides, g, into, part, parts):
    rows, half = w[0].shape
    half_cols = half // TILE
    whole, _, _, _ = right_specs(rows, 0, half_cols)
    _, full, _, _ = right_specs(rows, part, half_cols)
    prior = [] if into is None else [into]
    return pl.pallas_call(
        right_last_kernel,
        grid=(2 * half_cols,),
        in_specs=[BAND, BAND, whole(HALO), whole(half), whole(half), whole(HALO), full]
        + [pl.BlockSpec(memory_space=pl.ANY)] * len(prior),
        out_specs=full,
        scratch_shapes=[pltpu.VMEM((rows, 2 * (half + HALO)), jnp.bfloat16)] * 2,
        out_shape=jax.ShapeDtypeStruct((rows * parts, 2 * half), jnp.float32),
        input_output_aliases={7: 0} if prior else {},
        compiler_params=params(),
        cost_estimate=cost(6 * rows * 2 * half * WIDE, 5 * rows * 2 * half * 4),
    )(*bands, sides[0], *w, sides[1], g, *prior)


def permute(array, moves):
    return lax.ppermute(array, "row", moves)


def permute_by_column(array, moves):
    cols = lax.axis_size("col")
    pairs = [
        (source * cols + col, target * cols + col)
        for col in range(cols)
        for source, target in moves(col)
    ]
    return lax.ppermute(array, ("row", "col"), pairs)


def dev(chip, core):
    return 2 * chip + core


def after(value, *others):
    return lax.optimization_barrier((value, *others))[0]


def off_chip_rows(x):
    count = lax.axis_size("row")
    moves = []
    for low in range(1, count - 1, 2):
        moves += [(low, low + 1), (low + 1, low)]
    straight = [pair for pair in moves if set(pair) != {dev(1, 1), dev(2, 0)}]
    first = permute(x[0], moves)
    hop = permute(x[1], [(dev(1, 1), dev(3, 1)), (dev(2, 0), dev(0, 0))])
    second = permute(x[1], straight)
    return first, second, hop


def relay(hop):
    return permute(hop, [(dev(3, 1), dev(2, 0)), (dev(0, 0), dev(1, 1))])


def sides(low_half, high_half):
    cols = lax.axis_size("col")
    low_side = lax.ppermute(high_half, "col", [(i, i + 1) for i in range(cols - 1)])
    high_side = lax.ppermute(low_half, "col", [(i + 1, i) for i in range(cols - 1)])
    return low_side, high_side


def halves(x):
    middle = x.shape[1] // 2
    return lax.slice_in_dim(x, 0, middle, axis=1), lax.slice_in_dim(x, middle, None, axis=1)


def paired_body(p_cov, a_blocks, pattern, q_diag):
    rows_dev, cols_dev = p_cov.shape
    row = lax.axis_index("row")
    col = lax.axis_index("col")
    chip = row // 2
    at_core = lax.rem(row, 2)
    core = jnp.full((1,), at_core, jnp.int32)
    relayed = ((row == dev(1, 1)) | (row == dev(2, 0))).astype(jnp.int32)
    offset = col * cols_dev - row * rows_dev
    where = [
        jnp.stack([at_core, offset + half * HALO, relayed * half]).astype(jnp.int32)
        for half in (0, 1)
    ]
    count = lax.axis_size("row")
    swap = [(i, i ^ 1) for i in range(count)]
    noise = q_diag.reshape(rows_dev, 1)
    col_count = cols_dev // BS

    all_slots = lax.all_gather(pattern, "row", axis=0, tiled=True)
    place = jnp.stack([row * (rows_dev // BS), at_core]).astype(jnp.int32)
    near_bands, far_bands = row_bands(a_blocks, pattern, place)

    p_sent = after(p_cov, all_slots)
    sibling = permute(p_sent, swap)
    p = halves(p_sent)
    first, straight, hop = off_chip_rows(p)
    p_far = ((first, first), (straight, relay(hop)))
    p_sides = sides(*p)
    m_near = near(core, near_bands, [p_cov], [sibling], time_step)

    def far_of_p(h, far):
        return far_part(where[h], far_bands, far, noise, [m_near], h * HALO, time_step, True)

    away = chip ^ col
    by_core = jnp.array([[0, 1, 2, 3], [0, 4, 1, 3]], jnp.int32)
    role = by_core[at_core, away].reshape(1)
    size = a_blocks.shape[0] // CHUNKS
    owns = [lax.slice_in_dim(a_blocks, k * size, (k + 1) * size, axis=0) for k in range(CHUNKS)]
    owns = [after(own, all_slots) for own in owns]
    ones = [
        permute_by_column(own, lambda c: [(dev(c, 0), dev(c ^ 1, 0)), (dev(c, 1), dev(c ^ 2, 1))])
        for own in owns
    ]
    twos = [permute_by_column(own, lambda c: [(dev(c, 0), dev(c ^ 2, 0))]) for own in owns]
    ones = [after(ones[0], sibling), after(ones[1], m_near)]
    seconds = [
        permute_by_column(
            one, lambda c: [(dev(c ^ 1, 0), dev(c ^ 3, 0)), (dev(c ^ 2, 1), dev(c ^ 3, 1))]
        )
        for one in ones
    ]
    thirds = [
        permute_by_column(second, lambda c: [(dev(c ^ 3, 1), dev(c ^ 1, 1))])
        for second in (after(seconds[0], m_near), seconds[1])
    ]
    p_far = [
        [after(part, *held) for part in parts]
        for parts, held in zip(p_far, (seconds[:1], (thirds[0], *twos, *p_sides)))
    ]
    m = [far_of_p(h, p_far[h]) for h in (0, 1)]
    m_sibling = [permute(part, swap) for part in m]
    m_first, m_second, m_hop = off_chip_rows(m)
    half_step = 0.5 * time_step

    forced_mine = ((m[0],), (m[1],))
    mines, others = [], []
    for chunk in range(CHUNKS):
        own = after(owns[chunk], *forced_mine[chunk])
        mines.append(pick(role, own, ones[chunk], twos[chunk], seconds[chunk], thirds[chunk]))
        others.append(permute(mines[chunk], swap))
    bands = ()
    for chunk in range(CHUNKS):
        first_rows = [col * col_count + half * (col_count // 2) + chunk * size for half in (0, 1)]
        slots = jnp.concatenate(
            [lax.dynamic_slice_in_dim(all_slots, row_at, size, axis=0) for row_at in first_rows], axis=0
        )
        base = jnp.stack(first_rows).astype(jnp.int32)
        bands = col_bands(mines[chunk], others[chunk], slots, base, core, chunk, bands)

    parts = 2
    got = []
    for part in range(parts):
        shift = where[0] - jnp.array([0, part * (rows_dev // parts), 0], jnp.int32)
        noise_then = after(noise, m_sibling[1]) if part else noise
        got.append(right_first(shift, bands, p_cov, p_sides, m, noise_then, part, parts))
    w_sides = [sides(w_low, w_high) for w_low, w_high, _ in got]
    bases = [base for _, _, base in got]
    m_landed = relay(after(m_hop, bases[0]))
    g = near(core, near_bands, m, m_sibling, half_step, bases)
    g = far_part(where[0], far_bands, (m_first, m_first), noise, [g], 0, half_step, False, True)
    out = None
    for part in range(parts):
        out = right_last(bands, got[part][:2], w_sides[part], g, out, part, parts)
    return far_part(where[1], far_bands, (m_second, m_landed), noise, [out], HALO, half_step, False, True)


def solution(mesh):
    def body(p_cov, a_blocks, pattern, q_diag):
        rows_dev, cols_dev = p_cov.shape
        rows, cols = lax.axis_size("row"), lax.axis_size("col")
        paired = rows == 8 and cols == 4 and rows_dev == HALO and cols_dev == 2 * HALO
        return (paired_body if paired else general_body)(p_cov, a_blocks, pattern, q_diag)

    return jax.shard_map(
        body,
        mesh=mesh,
        in_specs=(P("row", "col"), P("row", None, None, None), P("row", None), P("row")),
        out_specs=P("row", "col"),
        check_vma=False,
    )
```
